32 devices in a mesh: grp: 4 (over z), tp: 8 (over y, x, core).
Axes of the slice: x: 2, y: 2, z: 4, core: 2. Of those that a mesh axis runs over, the one named last changes fastest.
Arguments:
- hidden: bfloat16 [1024, 8192], P('grp'), may hold values from -30 to 30
- proj_weight: bfloat16 [8192, 8192], P(None, 'tp'), may hold values from -0.32040776 to 0.32040776
- proj_bias: float32 [8192], P('tp'), may hold values from -3 to 3
- tile_pos: int32 [128], replicated, may hold values from 0 to 383, as said below
- text_embed: bfloat16 [3072, 8192], P('grp', 'tp'), may hold values from -76 to 76
- norm_gain: float32 [8192], P('tp'), may hold values from 0.25 to 1.75
- d_normed: bfloat16 [3072, 8192], P('grp', 'tp'), may hold values from -6 to 6
Outputs:
- normed: bfloat16 [3072, 8192], P('grp', 'tp')
- d_text: bfloat16 [3072, 8192], P('grp', 'tp')
- d_hidden: bfloat16 [1024, 8192], P('grp', 'tp')
The draws below stay inside these ranges and needn't reach their ends.
Inputs may be any that keep to these rules, and one draw needn't show every extreme that they name: `tile_pos`: all positions are distinct. Of the tiles k * 32 to (k + 1) * 32 - 1, at most 8 lie in the 96 tile positions of one index of grp, and in every draw each such block has exactly 8 tiles in some index of grp.
All inputs are finite; a program needn't handle non-finite values.
Results may differ from the reference program's by a relative error of at most 0.015.
Values may be sent and summed in bfloat16 or wider, within the bound.
A program may use at most 64 MiB of HBM per device.

```python
import math
import jax
import jax.numpy as jnp
from jax import lax

D = 8192
TILE = 8
TILES_DEV = 32
TPD = 96
CAP = 8
NTILE = 128
IMG_ROWS = 1024
TOKENS = 3072
N_GRP = 4
N_TP = 8


def col_profile(key_cols, span_width):
    rising = 10.0 ** (jnp.arange(span_width, dtype=jnp.float32) / span_width - 0.5)
    jitter = jnp.exp(jax.random.uniform(key_cols, (span_width,), jnp.float32, -0.4, 0.4))
    return rising * jitter


def row_profile(key_rows, count_rows, lowest, highest):
    return jnp.exp(jax.random.uniform(key_rows, (count_rows, 1), jnp.float32, math.log(lowest), math.log(highest)))


def draw_hidden(key, part):
    key_rows, key_cols, key_vals = jax.random.split(jax.random.fold_in(key, 11), 3)
    scales = row_profile(key_rows, IMG_ROWS, 0.5, 5.0)
    entries = jnp.clip(jax.random.normal(key_vals, (IMG_ROWS, D), jnp.float32), -4.0, 4.0)
    jitter = jnp.exp(jax.random.uniform(key_cols, (1, D), jnp.float32, -0.4, 0.4))
    return (entries * scales * jitter).astype(jnp.bfloat16)


def draw_proj_weight(key, part):
    key_cols, key_vals = jax.random.split(jax.random.fold_in(key, 23), 2)
    scales = col_profile(key_cols, D)[None, :] / math.sqrt(D)
    entries = jnp.clip(jax.random.normal(key_vals, (D, D), jnp.float32), -4.0, 4.0)
    return (entries * scales).astype(jnp.bfloat16)


def draw_text_embed(key, part):
    key_rows, key_cols, key_vals = jax.random.split(jax.random.fold_in(key, 37), 3)
    scales = row_profile(key_rows, TOKENS, 0.3, 3.0)
    columns = col_profile(key_cols, D)[None, :]
    entries = jnp.clip(jax.random.normal(key_vals, (TOKENS, D), jnp.float32), -4.0, 4.0)
    return (entries * scales * columns).astype(jnp.bfloat16)


def draw_tile_pos(key, part):
    key_offsets, key_starts = jax.random.split(jax.random.fold_in(key, 53), 2)
    fanout = TILES_DEV // CAP
    offsets = jax.random.permutation(key_offsets, N_GRP).astype(jnp.int32)[:fanout]
    starts = jax.random.randint(key_starts, (N_GRP,), 0, TPD - TILES_DEV + 1, dtype=jnp.int32)
    tile_index = jnp.arange(NTILE, dtype=jnp.int32)
    source = tile_index // TILES_DEV
    within = tile_index % TILES_DEV
    target = (source + offsets[within // CAP]) % N_GRP
    return (target * TPD + starts[target] + within).astype(jnp.int32)


def block_levels(stream_key, dims, pieces, least, high):
    loudness, own = 1.0, jax.random.fold_in(stream_key, 6)
    for position, blocks in pieces:
        draws = jnp.exp(jax.random.uniform(jax.random.fold_in(own, position), (blocks,), jnp.float32, least / len(pieces), high / len(pieces)))
        loudness = loudness * jnp.repeat(draws, dims[position] // blocks).reshape([-1 if axis == position else 1 for axis in range(len(dims))])
    return loudness


def centred(own_key, dims, deviation, limit, shards=(), kind=jnp.bfloat16):
    values = deviation * jax.random.normal(own_key, dims, jnp.float32)
    if shards:
        values = values * block_levels(own_key, dims, shards, -0.22, 0.18)
    return jnp.clip(values, -limit, limit).astype(kind)


def setup_inputs(seed: int = 0) -> dict:
    key_list = jax.random.split(jax.random.key(seed), 8)
    hidden = draw_hidden(jax.random.fold_in(key_list[7], 71), 0)
    proj_weight = draw_proj_weight(jax.random.fold_in(key_list[7], 71), 0)
    proj_bias = centred(key_list[2], (D,), 0.5, 3.0, ((0, 8),), jnp.float32)
    tile_pos = draw_tile_pos(jax.random.fold_in(key_list[7], 71), 0)
    text_embed = draw_text_embed(jax.random.fold_in(key_list[7], 71), 0)
    norm_gain = jnp.clip(1.0 + 0.15 * jax.random.normal(key_list[5], (D,), jnp.float32), 0.25, 1.75)
    d_normed = centred(key_list[6], (TOKENS, D), 1.0, 6.0, ((0, 4), (1, 8)))
    return {"hidden": hidden, "proj_weight": proj_weight, "proj_bias": proj_bias, "tile_pos": tile_pos, "text_embed": text_embed, "norm_gain": norm_gain, "d_normed": d_normed}


epsilon = 1e-05

def gelu_slope(values):
    normal_cdf = 0.5 * (1.0 + lax.erf(values * 0.7071067811865476))
    density = jnp.exp(-0.5 * values * values) * 0.3989422804014327
    return normal_cdf + values * density

def reference(hidden, proj_weight, proj_bias, tile_pos, text_embed, norm_gain, d_normed):
    hidden_wide = hidden.astype(jnp.float32)
    activated = jax.nn.gelu(hidden_wide, approximate=False).astype(jnp.bfloat16)
    image_rows = (jnp.dot(activated, proj_weight, preferred_element_type=jnp.float32) + proj_bias).astype(jnp.bfloat16)
    document = text_embed.reshape(TOKENS // TILE, TILE * D)
    merged = document.at[tile_pos].set(image_rows.reshape(NTILE, TILE * D)).reshape(TOKENS, D)
    is_image = jnp.zeros((TOKENS // TILE,), jnp.float32).at[tile_pos].set(1.0)
    wide_merged = merged.astype(jnp.float32)
    inverse = lax.rsqrt(lax.optimization_barrier(jnp.mean(wide_merged * wide_merged, axis=1, keepdims=True)) + epsilon)
    normed = (wide_merged * inverse * norm_gain).astype(jnp.bfloat16)
    grad_in = d_normed.astype(jnp.float32) * norm_gain
    cross_mean = lax.optimization_barrier(jnp.mean(grad_in * wide_merged, axis=1, keepdims=True))
    d_merged = inverse * (grad_in - wide_merged * inverse * inverse * cross_mean)
    d_tiles = d_merged.reshape(TOKENS // TILE, TILE * D)
    d_text = jnp.where(is_image[:, None] > 0.5, 0.0, d_tiles).astype(jnp.bfloat16).reshape(TOKENS, D)
    d_image = d_tiles[tile_pos].astype(jnp.bfloat16).reshape(IMG_ROWS, D)
    blocks = D // N_TP

    def add_block(running, block_index):
        columns = lax.dynamic_slice_in_dim(d_image, block_index * blocks, blocks, 1)
        weights = lax.dynamic_slice_in_dim(proj_weight, block_index * blocks, blocks, 1)
        partial_value = lax.dot_general(columns, weights, (((1,), (1,)), ((), ())), preferred_element_type=jnp.float32)
        partial_value = lax.optimization_barrier(partial_value.astype(jnp.bfloat16)).astype(jnp.float32)
        return (running + partial_value, None)
    d_act, _ = lax.scan(add_block, jnp.zeros((IMG_ROWS, D), jnp.float32), jnp.arange(N_TP, dtype=jnp.int32))
    d_hidden = (d_act * gelu_slope(hidden_wide)).astype(jnp.bfloat16)
    return (normed, d_text, d_hidden)
```

```python
import functools

import jax
import jax.numpy as jnp
from jax import lax
from jax.experimental import pallas as pl
from jax.experimental.pallas import tpu as pltpu
from jax.sharding import PartitionSpec as P

TILE = 8
STRIP = 2 * TILE
LANES = 128
MESH = pl.DeviceIdType.MESH
F32 = jnp.float32
BF16 = jnp.bfloat16

epsilon = 1e-05


def normal_cdf(values):
    return 0.5 * (1.0 + lax.erf(values * 0.7071067811865476))


def gelu_slope(values):
    density = jnp.exp(-0.5 * values * values) * 0.3989422804014327
    return normal_cdf(values) + values * density


def tile_maps(tile_pos, groups, tiles_dev, spread, capacity):
    group_index = lax.axis_index("grp")
    slots = groups * capacity
    tile_index = jnp.arange(tile_pos.shape[0], dtype=jnp.int32)
    source = tile_index // tiles_dev
    target = tile_pos // spread
    local_pos = tile_pos - group_index * spread
    earlier = (
        (source[:, None] == source[None, :])
        & (target[:, None] == target[None, :])
        & (tile_index[None, :] < tile_index[:, None])
    )
    standing = jnp.sum(earlier.astype(jnp.int32), axis=1)
    arrive = source * capacity + standing
    here = target == group_index
    slot_index = jnp.arange(slots, dtype=jnp.int32)
    needed = jnp.sum(
        jnp.where(here[None, :] & (arrive[None, :] == slot_index[:, None]), local_pos[None, :], 0),
        axis=1,
    )
    depart = target * capacity + standing
    mine = source == group_index
    own_slot = lax.dynamic_slice_in_dim(depart, group_index * tiles_dev, tiles_dev, 0)
    tile_of_slot = jnp.sum(
        jnp.where(
            mine[None, :] & (depart[None, :] == slot_index[:, None]),
            (tile_index - group_index * tiles_dev)[None, :],
            0,
        ),
        axis=1,
    )
    hits = local_pos[None, :] == jnp.arange(spread, dtype=jnp.int32)[:, None]
    place = jnp.sum(jnp.where(hits, arrive[None, :] + 1, 0), axis=1) - 1
    return jnp.concatenate([needed, own_slot, tile_of_slot, place])


def halving_plan(lanes):
    bits = lanes.bit_length() - 1
    orders = (list(range(1, bits)), list(range(bits - 1, 0, -1)))
    plan = []
    for order in orders:
        kept = [rel for rel in range(lanes) if rel % 2 == 0]
        stages = []
        number = 0
        for bit in order:
            sent = [rel for rel in kept if (rel >> bit) & 1]
            kept = [rel for rel in kept if not (rel >> bit) & 1]
            stages.append((bit, {rel: number + place for place, rel in enumerate(sent)}))
            number += len(sent)
        plan.append(stages)
    return plan


def kernel(
    groups, lanes, capacity,
    maps, hidden, weight, bias, gain, text, d_normed,
    normed_out, d_text_out, d_hidden_out,
    hid_v, w_v, act_v, acc_v, img_v, d_img_v, text_v, dn_v, normed_v, d_text_v, d_hid_v,
    send_dn, recv_dn, n_img, send_n, recv_n,
    stat_i, stat_x, row_i, row_x, got_i, got_x, coef_i, coef_x,
    part, first, later,
    load_sem, hid_sem, w_sem, out_sem,
    dn_s, dn_r, n_s, n_r, si_s, si_r, sx_s, sx_r, f_s, f_r, l_s, l_r,
):
    grp = lax.axis_index("grp")
    tp = lax.axis_index("tp")
    rows, cols = img_v.shape
    spread = text_v.shape[0]
    tiles_dev = rows // TILE
    slots = groups * capacity
    width = cols * lanes
    half = rows // 2
    piece = cols // 2 if cols % (2 * LANES) == 0 else cols
    at_slot, at_tile, at_place = slots, slots + tiles_dev, 2 * slots + tiles_dev

    def hid_copy(k):
        return pltpu.make_async_copy(
            hidden.at[:, pl.ds(pl.multiple_of(k * cols, cols), cols)], hid_v.at[k], hid_sem.at[k]
        )

    def w_copy(k):
        return pltpu.make_async_copy(
            weight.at[pl.ds(pl.multiple_of(k * cols, cols), cols), :], w_v.at[k], w_sem.at[k]
        )

    dn_copy = pltpu.make_async_copy(d_normed, dn_v, load_sem.at[0])
    text_copy = pltpu.make_async_copy(text, text_v, load_sem.at[1])
    dn_copy.start()
    hid_copy(0).start()
    w_copy(0).start()
    text_copy.start()
    for k in range(1, lanes):
        hid_copy(k).start()
        w_copy(k).start()

    barrier = pltpu.get_barrier_semaphore()
    for d in range(1, groups):
        pl.semaphore_signal(
            barrier, inc=1, device_id={"grp": (grp + d) % groups}, device_id_type=MESH
        )
    for d in range(1, lanes):
        pl.semaphore_signal(
            barrier, inc=1, device_id={"tp": (tp + d) % lanes}, device_id_type=MESH
        )

    def to_group(source, target, send, receive):
        copies = []
        for d in range(1, groups):
            peer = (grp + d) % groups
            copies.append(
                pltpu.make_async_remote_copy(
                    src_ref=source.at[pl.ds(peer * capacity, capacity)],
                    dst_ref=target.at[pl.ds(grp * capacity, capacity)],
                    send_sem=send.at[d - 1],
                    recv_sem=receive.at[d - 1],
                    device_id={"grp": peer},
                    device_id_type=MESH,
                )
            )
        return copies

    def to_lanes(source, target, send, receive):
        return [
            pltpu.make_async_remote_copy(
                src_ref=source,
                dst_ref=target.at[d - 1],
                send_sem=send.at[d - 1],
                recv_sem=receive.at[d - 1],
                device_id={"tp": (tp + d) % lanes},
                device_id_type=MESH,
            )
            for d in range(1, lanes)
        ]

    dn_copy.wait()

    @pl.loop(0, slots)
    def _(q):
        send_dn[q] = dn_v[maps[q]]

    @pl.loop(0, capacity)
    def _(k):
        recv_dn[grp * capacity + k] = dn_v[maps[grp * capacity + k]]

    pl.semaphore_wait(barrier, groups + lanes - 2)
    dn_copies = to_group(send_dn, recv_dn, dn_s, dn_r)
    for copy in dn_copies:
        copy.start()

    gains = gain[...]
    lane = lax.broadcasted_iota(jnp.int32, (STRIP, LANES), 1)

    def row_sums(values, grads):
        squares = jnp.sum(values * values, axis=1, keepdims=True)
        crosses = jnp.sum(grads * values, axis=1, keepdims=True)
        return jnp.where(lane == 0, squares, jnp.where(lane == 1, crosses, 0.0))

    def doc_strip(ref, j):
        return ref[pl.ds(2 * j, 2)].astype(F32).reshape(STRIP, cols)

    text_copy.wait()

    @pl.loop(0, spread // 2)
    def _(j):
        grads = doc_strip(dn_v, j) * gains
        stat_x[pl.ds(pl.multiple_of(j * STRIP, STRIP), STRIP), :] = row_sums(
            doc_strip(text_v, j), grads
        )

    row_x[...] = stat_x[...].T[:TILE, :]
    x_copies = to_lanes(row_x, got_x, sx_s, sx_r)
    for copy in x_copies:
        copy.start()

    acc_v[...] = jnp.zeros_like(acc_v)

    @pl.loop(0, lanes)
    def _(k):
        hid_copy(k).wait()

        @pl.loop(0, rows // STRIP)
        def _(j):
            strip = pl.ds(pl.multiple_of(j * STRIP, STRIP), STRIP)
            values = hid_v[k, strip, :].astype(F32)
            act_v[strip, :] = (values * normal_cdf(values)).astype(BF16)

        w_copy(k).wait()

        @pl.loop(0, cols // piece)
        def _(n):
            span = pl.ds(pl.multiple_of(n * piece, LANES), piece)
            acc_v[:, span] += jnp.dot(act_v[...], w_v[k, :, span], preferred_element_type=F32)

    for copy in dn_copies:
        copy.wait_recv()

    def grad_strip(j):
        one = recv_dn[maps[at_slot + 2 * j]].astype(F32)
        two = recv_dn[maps[at_slot + 2 * j + 1]].astype(F32)
        return jnp.concatenate([one, two], axis=0) * gains

    biases = bias[...]

    @pl.loop(0, rows // STRIP)
    def _(j):
        strip = pl.ds(pl.multiple_of(j * STRIP, STRIP), STRIP)
        image = (acc_v[strip, :] + biases).astype(BF16)
        img_v[strip, :] = image
        stat_i[strip, :] = row_sums(image.astype(F32), grad_strip(j))

    row_i[...] = stat_i[...].T[:TILE, :]
    i_copies = to_lanes(row_i, got_i, si_s, si_r)
    for copy in i_copies:
        copy.start()

    def coefficients(own, got, copies, target):
        for copy in copies:
            copy.wait_recv()
        total = own[...]
        for d in range(lanes - 1):
            total = total + got[d]
        inverse = lax.rsqrt(total[0:1, :] / width + epsilon)
        second = inverse * inverse * (total[1:2, :] / width)
        count = own.shape[1]
        stacked = jnp.concatenate(
            [
                jnp.broadcast_to(inverse, (TILE, count)),
                jnp.broadcast_to(second, (TILE, count)),
                jnp.zeros((LANES - 2 * TILE, count), F32),
            ],
            axis=0,
        )
        target[...] = stacked.T

    coefficients(row_i, got_i, i_copies, coef_i)

    @pl.loop(0, rows // STRIP)
    def _(j):
        strip = pl.ds(pl.multiple_of(j * STRIP, STRIP), STRIP)
        image = img_v[strip, :].astype(F32)
        inverse = coef_i[strip, 0:1]
        second = coef_i[strip, TILE : TILE + 1]
        d_img_v[strip, :] = (inverse * (grad_strip(j) - image * second)).astype(BF16)
        n_img[pl.ds(2 * j, 2)] = (image * inverse * gains).reshape(2, TILE, cols).astype(BF16)

    @pl.loop(0, slots)
    def _(q):
        send_n[q] = n_img[maps[at_tile + q]]

    @pl.loop(0, capacity)
    def _(k):
        recv_n[grp * capacity + k] = n_img[maps[at_tile + grp * capacity + k]]

    n_copies = to_group(send_n, recv_n, n_s, n_r)
    for copy in n_copies:
        copy.start()

    bit_steps = []
    left = tp
    for bit in range(lanes.bit_length() - 1):
        bit_steps.append((1 - 2 * (left % 2)) * (1 << bit))
        left = left // 2
    plan = halving_plan(lanes)

    def block_of(rel):
        block = tp
        for bit, step in enumerate(bit_steps):
            if (rel >> bit) & 1:
                block = block + step
        return block

    def product(rel, add):
        block = block_of(rel)

        @pl.loop(0, cols // piece)
        def _(n):
            span = pl.ds(pl.multiple_of(n * piece, LANES), piece)
            value = lax.dot_general(
                d_img_v[...], w_v[block, span, :], (((1,), (1,)), ((), ())),
                preferred_element_type=F32,
            )
            if add is not None:
                value = value + first[add, :, span].astype(F32)
            part[rel, :, span] = value.astype(BF16)

    def first_copy(rel):
        return pltpu.make_async_remote_copy(
            src_ref=part.at[rel],
            dst_ref=first.at[rel // 2],
            send_sem=f_s.at[rel // 2],
            recv_sem=f_r.at[rel // 2],
            device_id={"tp": tp + bit_steps[0]},
            device_id_type=MESH,
        )

    def later_copy(side, bit, rel, number):
        return pltpu.make_async_remote_copy(
            src_ref=part.at[rel, pl.ds(side * half, half), :],
            dst_ref=later.at[side, number],
            send_sem=l_s.at[side, number],
            recv_sem=l_r.at[side, number],
            device_id={"tp": tp + bit_steps[bit]},
            device_id_type=MESH,
        )

    urgent = sorted(range(0, lanes, 2), key=lambda rel: (-bin(rel).count("1"), -rel))
    first_copies = {}
    later_copies = {}
    for rel in urgent:
        product(rel + 1, None)
        first_copies[rel] = first_copy(rel + 1)
        first_copies[rel].start()

    def send_on(side, stage, rel):
        if stage < len(plan[side]) and rel in plan[side][stage][1]:
            bit, numbers = plan[side][stage]
            copy = later_copy(side, bit, rel, numbers[rel])
            later_copies[side, numbers[rel]] = copy
            copy.start()

    for rel in urgent:
        first_copies[rel].wait_recv()
        product(rel, rel // 2)
        for side in range(2):
            send_on(side, 0, rel)

    coefficients(row_x, got_x, x_copies, coef_x)

    @pl.loop(0, spread // 2)
    def _(j):
        strip = pl.ds(pl.multiple_of(j * STRIP, STRIP), STRIP)
        values = doc_strip(text_v, j)
        grads = doc_strip(dn_v, j) * gains
        inverse = coef_x[strip, 0:1]
        second = coef_x[strip, TILE : TILE + 1]
        normed_v[pl.ds(2 * j, 2)] = (
            (values * inverse * gains).reshape(2, TILE, cols).astype(BF16)
        )
        d_values = inverse * (grads - values * second)
        for side in range(2):
            flag = jnp.full((TILE, cols), maps[at_place + 2 * j + side], jnp.int32)
            d_text_v[2 * j + side] = jnp.where(
                flag >= 0, 0.0, d_values[side * TILE : (side + 1) * TILE, :]
            ).astype(BF16)

    d_text_copy = pltpu.make_async_copy(d_text_v, d_text_out, out_sem.at[0])
    d_text_copy.start()

    @pl.loop(0, rows // STRIP)
    def _(j):
        strip = pl.ds(pl.multiple_of(j * STRIP, STRIP), STRIP)
        acc_v[strip, :] = gelu_slope(hid_v[tp, strip, :].astype(F32))

    def collect(stage, last):
        for side in range(2):
            if stage >= len(plan[side]):
                continue
            bit, numbers = plan[side][stage]
            ahead = plan[side][stage + 1][1] if stage + 1 < len(plan[side]) else {}
            goal = sorted(numbers, key=lambda rel: (rel - (1 << bit)) not in ahead)
            for rel in goal:
                number = numbers[rel]
                mine = rel - (1 << bit)
                later_copies[side, number].wait_recv()
                if mine:

                    @pl.loop(0, half // STRIP)
                    def _(j):
                        here = pl.multiple_of(j * STRIP, STRIP)
                        there = pl.ds(side * half + here, STRIP)
                        part[mine, there, :] = (
                            part[mine, there, :].astype(F32)
                            + later[side, number, pl.ds(here, STRIP), :].astype(F32)
                        ).astype(BF16)

                    send_on(side, stage + 1, mine)

    stages = len(plan[0])
    for stage in range(stages - 1):
        collect(stage, False)

    for copy in n_copies:
        copy.wait_recv()

    @pl.loop(0, spread)
    def _(p):
        slot = maps[at_place + p]
        flag = jnp.full((TILE, cols), slot, jnp.int32)
        normed_v[p] = jnp.where(
            flag >= 0, recv_n[jnp.maximum(slot, 0)].astype(F32), normed_v[p].astype(F32)
        ).astype(BF16)

    normed_copy = pltpu.make_async_copy(normed_v, normed_out, out_sem.at[1])
    normed_copy.start()
    if stages:
        collect(stages - 1, True)

    for side in range(2):
        tails = [numbers[1 << bit] for bit, numbers in plan[side]]

        @pl.loop(0, half // STRIP)
        def _(j):
            here = pl.multiple_of(j * STRIP, STRIP)
            there = pl.ds(side * half + here, STRIP)
            total = part[0, there, :].astype(F32)
            for number in tails:
                total = total + later[side, number, pl.ds(here, STRIP), :].astype(F32)
            d_hid_v[there, :] = (total * acc_v[there, :]).astype(BF16)

    d_hidden_copy = pltpu.make_async_copy(d_hid_v, d_hidden_out, out_sem.at[2])
    d_hidden_copy.start()
    for copy in dn_copies + x_copies + i_copies + n_copies:
        copy.wait_send()
    for copy in list(first_copies.values()) + list(later_copies.values()):
        copy.wait_send()
    d_text_copy.wait()
    normed_copy.wait()
    d_hidden_copy.wait()


def on_device(hidden, proj_weight, proj_bias, tile_pos, text_embed, norm_gain, d_normed):
    rows, width = hidden.shape
    cols = proj_weight.shape[1]
    tokens = text_embed.shape[0]
    groups = lax.axis_size("grp")
    lanes = lax.axis_size("tp")
    assert lanes >= 2 and lanes & (lanes - 1) == 0, lanes
    tiles_dev = rows // TILE
    spread = tokens // TILE
    capacity = max(2, (tiles_dev + groups - 1) // groups)
    slots = groups * capacity
    maps = tile_maps(tile_pos, groups, tiles_dev, spread, capacity)
    any_spec = pl.BlockSpec(memory_space=pl.ANY)
    vmem_spec = pl.BlockSpec(memory_space=pltpu.VMEM)
    half = rows // 2
    kept = max(1, lanes // 2 - 1)

    def vmem(*shape, dtype=BF16):
        return pltpu.VMEM(shape, dtype)

    def sems(*shape):
        return pltpu.SemaphoreType.DMA(shape)

    tiled = (spread, TILE, cols)
    normed, d_text, d_hidden = pl.pallas_call(
        functools.partial(kernel, groups, lanes, capacity),
        out_shape=(
            jax.ShapeDtypeStruct(tiled, BF16),
            jax.ShapeDtypeStruct(tiled, BF16),
            jax.ShapeDtypeStruct((rows, cols), BF16),
        ),
        in_specs=[
            pl.BlockSpec(memory_space=pltpu.SMEM),
            any_spec, any_spec, vmem_spec, vmem_spec, any_spec, any_spec,
        ],
        out_specs=(any_spec, any_spec, any_spec),
        scratch_shapes=[
            vmem(lanes, rows, cols),
            vmem(lanes, cols, cols),
            vmem(rows, cols),
            vmem(rows, cols, dtype=F32),
            vmem(rows, cols),
            vmem(rows, cols),
            vmem(*tiled),
            vmem(*tiled),
            vmem(*tiled),
            vmem(*tiled),
            vmem(rows, cols),
            vmem(slots, TILE, cols),
            vmem(slots, TILE, cols),
            vmem(tiles_dev, TILE, cols),
            vmem(slots, TILE, cols),
            vmem(slots, TILE, cols),
            vmem(rows, LANES, dtype=F32),
            vmem(tokens, LANES, dtype=F32),
            vmem(TILE, rows, dtype=F32),
            vmem(TILE, tokens, dtype=F32),
            vmem(lanes - 1, TILE, rows, dtype=F32),
            vmem(lanes - 1, TILE, tokens, dtype=F32),
            vmem(rows, LANES, dtype=F32),
            vmem(tokens, LANES, dtype=F32),
            vmem(lanes, rows, cols),
            vmem(lanes // 2, rows, cols),
            vmem(2, kept, half, cols),
            sems(2), sems(lanes), sems(lanes), sems(3),
            sems(groups - 1), sems(groups - 1), sems(groups - 1), sems(groups - 1),
            sems(lanes - 1), sems(lanes - 1), sems(lanes - 1), sems(lanes - 1),
            sems(lanes // 2), sems(lanes // 2), sems(2, kept), sems(2, kept),
        ],
        compiler_params=pltpu.CompilerParams(
            collective_id=0, has_side_effects=True, vmem_limit_bytes=58 * 1024 * 1024
        ),
        cost_estimate=pl.CostEstimate(
            flops=4 * rows * width * cols,
            bytes_accessed=2 * (width * cols + rows * width + 5 * tokens * cols),
            transcendentals=rows * width,
        ),
        name="projector_norm",
    )(
        maps, hidden, proj_weight, proj_bias.reshape(1, cols), norm_gain.reshape(1, cols),
        text_embed.reshape(tiled), d_normed.reshape(tiled),
    )
    return (normed.reshape(tokens, cols), d_text.reshape(tokens, cols), d_hidden)


def solution(mesh):
    in_specs = (
        P("grp", None),
        P(None, "tp"),
        P("tp"),
        P(),
        P("grp", "tp"),
        P("tp"),
        P("grp", "tp"),
    )
    out_specs = (P("grp", "tp"), P("grp", "tp"), P("grp", "tp"))
    return jax.shard_map(
        on_device, mesh=mesh, in_specs=in_specs, out_specs=out_specs, check_vma=False
    )
```

```python
import functools

import jax
import jax.numpy as jnp
from jax import lax
from jax.experimental import pallas as pl
from jax.experimental.pallas import tpu as pltpu
from jax.sharding import PartitionSpec as P

TILE = 8
STRIP = 2 * TILE
LANES = 128
MESH = pl.DeviceIdType.MESH
F32 = jnp.float32
BF16 = jnp.bfloat16

epsilon = 1e-05


def normal_cdf(values):
    return 0.5 * (1.0 + lax.erf(values * 0.7071067811865476))


def gelu_slope(values):
    density = jnp.exp(-0.5 * values * values) * 0.3989422804014327
    return normal_cdf(values) + values * density


def tile_maps(tile_pos, groups, tiles_dev, spread, capacity):
    group_index = lax.axis_index("grp")
    slots = groups * capacity
    tile_index = jnp.arange(tile_pos.shape[0], dtype=jnp.int32)
    source = tile_index // tiles_dev
    target = lax.div(tile_pos, jnp.int32(spread))
    local_pos = tile_pos - group_index * spread
    earlier = (
        (source[:, None] == source[None, :])
        & (target[:, None] == target[None, :])
        & (tile_index[None, :] < tile_index[:, None])
    )
    standing = jnp.sum(earlier.astype(jnp.int32), axis=1)
    arrive = source * capacity + standing
    here = target == group_index
    slot_index = jnp.arange(slots, dtype=jnp.int32)
    needed = jnp.sum(
        jnp.where(here[None, :] & (arrive[None, :] == slot_index[:, None]), local_pos[None, :], 0),
        axis=1,
    )
    depart = target * capacity + standing
    mine = source == group_index
    own_slot = lax.dynamic_slice_in_dim(depart, group_index * tiles_dev, tiles_dev, 0)
    tile_of_slot = jnp.sum(
        jnp.where(
            mine[None, :] & (depart[None, :] == slot_index[:, None]),
            (tile_index - group_index * tiles_dev)[None, :],
            0,
        ),
        axis=1,
    )
    hits = local_pos[None, :] == jnp.arange(spread, dtype=jnp.int32)[:, None]
    place = jnp.sum(jnp.where(hits, arrive[None, :] + 1, 0), axis=1) - 1
    return jnp.concatenate([needed, own_slot, tile_of_slot, place])


def halving_plan(lanes):
    bits = lanes.bit_length() - 1
    orders = (list(range(1, bits)), list(range(bits - 1, 0, -1)))
    plan = []
    for order in orders:
        kept = [rel for rel in range(lanes) if rel % 2 == 0]
        stages = []
        number = 0
        for bit in order:
            sent = [rel for rel in kept if (rel >> bit) & 1]
            kept = [rel for rel in kept if not (rel >> bit) & 1]
            stages.append((bit, {rel: number + place for place, rel in enumerate(sent)}))
            number += len(sent)
        plan.append(stages)
    return plan


def kernel(
    groups, lanes, capacity,
    maps, hidden, weight, bias, gain, text, d_normed,
    normed_v, d_text_v, d_hid_v,
    hid_v, w_v, act_v, act_got, acc_v, img_v, d_img_v, text_v, dn_v,
    send_dn, recv_dn, n_img, send_n, recv_n,
    stat_i, stat_x, row_i, row_x, got_i, got_x, coef_i, coef_x,
    part, first, later,
    load_sem, hid_sem, w_sem, a_s, a_r,
    dn_s, dn_r, n_s, n_r, si_s, si_r, sx_s, sx_r, f_s, f_r, l_s, l_r,
):
    grp = lax.axis_index("grp")
    tp = lax.axis_index("tp")
    rows, cols = img_v.shape
    spread = text_v.shape[0]
    tiles_dev = rows // TILE
    slots = groups * capacity
    width = cols * lanes
    half = rows // 2
    piece = cols // 2 if cols % (2 * LANES) == 0 else cols
    at_slot, at_tile, at_place = slots, slots + tiles_dev, 2 * slots + tiles_dev

    odd = tp % 2
    pairs = lanes // 2

    def hid_copy(k):
        return pltpu.make_async_copy(
            hidden.at[:, pl.ds(pl.multiple_of((2 * k + odd) * cols, cols), cols)],
            hid_v.at[k],
            hid_sem.at[k],
        )

    def w_copy(k, other):
        block = 2 * k + (1 - odd if other else odd)
        return pltpu.make_async_copy(
            weight.at[pl.ds(pl.multiple_of(block * cols, cols), cols), :],
            w_v.at[block],
            w_sem.at[2 * k + other],
        )

    dn_copy = pltpu.make_async_copy(d_normed, dn_v, load_sem.at[0])
    text_copy = pltpu.make_async_copy(text, text_v, load_sem.at[1])
    dn_copy.start()
    hid_copy(0).start()
    w_copy(0, 0).start()
    for k in range(1, pairs):
        hid_copy(k).start()
        w_copy(k, 0).start()
        w_copy(k - 1, 1).start()
    w_copy(pairs - 1, 1).start()
    text_copy.start()

    barrier = pltpu.get_barrier_semaphore()
    for d in range(1, groups):
        pl.semaphore_signal(
            barrier, inc=1, device_id={"grp": (grp + d) % groups}, device_id_type=MESH
        )
    for d in range(1, lanes):
        pl.semaphore_signal(
            barrier, inc=1, device_id={"tp": (tp + d) % lanes}, device_id_type=MESH
        )

    def to_group(source, target, send, receive):
        copies = []
        for d in range(1, groups):
            peer = (grp + d) % groups
            copies.append(
                pltpu.make_async_remote_copy(
                    src_ref=source.at[pl.ds(peer * capacity, capacity)],
                    dst_ref=target.at[pl.ds(grp * capacity, capacity)],
                    send_sem=send.at[d - 1],
                    recv_sem=receive.at[d - 1],
                    device_id={"grp": peer},
                    device_id_type=MESH,
                )
            )
        return copies

    def to_lanes(source, target, send, receive):
        return [
            pltpu.make_async_remote_copy(
                src_ref=source,
                dst_ref=target.at[d - 1],
                send_sem=send.at[d - 1],
                recv_sem=receive.at[d - 1],
                device_id={"tp": (tp + d) % lanes},
                device_id_type=MESH,
            )
            for d in range(1, lanes)
        ]

    dn_copy.wait()

    @pl.loop(0, slots)
    def _(q):
        send_dn[q] = dn_v[maps[q]]

    @pl.loop(0, capacity)
    def _(k):
        recv_dn[grp * capacity + k] = dn_v[maps[grp * capacity + k]]

    pl.semaphore_wait(barrier, groups + lanes - 2)
    dn_copies = to_group(send_dn, recv_dn, dn_s, dn_r)
    for copy in dn_copies:
        copy.start()

    gains = gain[...]
    lane = lax.broadcasted_iota(jnp.int32, (STRIP, LANES), 1)

    def row_sums(values, grads):
        squares = jnp.sum(values * values, axis=1, keepdims=True)
        crosses = jnp.sum(grads * values, axis=1, keepdims=True)
        return jnp.where(lane == 0, squares, jnp.where(lane == 1, crosses, 0.0))

    def doc_strip(ref, j):
        return ref[pl.ds(2 * j, 2)].astype(F32).reshape(STRIP, cols)

    bit_steps = []
    left = tp
    for bit in range(lanes.bit_length() - 1):
        bit_steps.append((1 - 2 * (left % 2)) * (1 << bit))
        left = left // 2

    act_copies = [
        pltpu.make_async_remote_copy(
            src_ref=act_v.at[k],
            dst_ref=act_got.at[k],
            send_sem=a_s.at[k],
            recv_sem=a_r.at[k],
            device_id={"tp": tp + bit_steps[0]},
            device_id_type=MESH,
        )
        for k in range(pairs)
    ]
    steps = min(4, cols // LANES)
    span_width = cols // steps
    strips = rows // STRIP // steps

    def forward(k, ready):
        if k is not None:
            hid_copy(k).wait()
        for source, other in ready:
            w_copy(source, other).wait()
            if other:
                act_copies[source].wait_recv()

        @pl.loop(0, steps)
        def _(n):
            if k is not None:
                for j in range(strips):
                    strip = pl.ds(pl.multiple_of((n * strips + j) * STRIP, STRIP), STRIP)
                    values = hid_v[k, strip, :].astype(F32)
                    act_v[k, strip, :] = (values * normal_cdf(values)).astype(BF16)
            if ready:
                span = pl.ds(pl.multiple_of(n * span_width, LANES), span_width)
                total = None if ready[0] == (0, 0) else acc_v[:, span]
                for source, other in ready:
                    block = 2 * source + (1 - odd if other else odd)
                    left_side = act_got[source] if other else act_v[source]
                    value = jnp.dot(
                        left_side, w_v[block, :, span], preferred_element_type=F32
                    )
                    total = value if total is None else total + value
                acc_v[:, span] = total

        if k is not None:
            act_copies[k].start()

    for k in range(pairs):
        ready = []
        if k >= 1:
            ready.append((k - 1, 0))
        if k >= 2:
            ready.append((k - 2, 1))
        forward(k, ready)
    tail = [(pairs - 1, 0)]
    if pairs >= 2:
        tail.append((pairs - 2, 1))
    forward(None, tail)
    forward(None, [(pairs - 1, 1)])

    for copy in dn_copies:
        copy.wait_recv()

    def grad_strip(j):
        one = recv_dn[maps[at_slot + 2 * j]].astype(F32)
        two = recv_dn[maps[at_slot + 2 * j + 1]].astype(F32)
        return jnp.concatenate([one, two], axis=0) * gains

    biases = bias[...]

    @pl.loop(0, rows // STRIP)
    def _(j):
        strip = pl.ds(pl.multiple_of(j * STRIP, STRIP), STRIP)
        image = (acc_v[strip, :] + biases).astype(BF16)
        img_v[strip, :] = image
        stat_i[strip, :] = row_sums(image.astype(F32), grad_strip(j))

    row_i[...] = stat_i[...].T[:TILE, :]
    i_copies = to_lanes(row_i, got_i, si_s, si_r)
    for copy in i_copies:
        copy.start()

    text_copy.wait()

    @pl.loop(0, spread // 2)
    def _(j):
        grads = doc_strip(dn_v, j) * gains
        stat_x[pl.ds(pl.multiple_of(j * STRIP, STRIP), STRIP), :] = row_sums(
            doc_strip(text_v, j), grads
        )

    row_x[...] = stat_x[...].T[:TILE, :]
    x_copies = to_lanes(row_x, got_x, sx_s, sx_r)
    for copy in x_copies:
        copy.start()

    def coefficients(own, got, copies, target):
        for copy in copies:
            copy.wait_recv()
        total = own[...]
        for d in range(lanes - 1):
            total = total + got[d]
        inverse = lax.rsqrt(total[0:1, :] / width + epsilon)
        second = inverse * inverse * (total[1:2, :] / width)
        count = own.shape[1]
        stacked = jnp.concatenate(
            [
                jnp.broadcast_to(inverse, (TILE, count)),
                jnp.broadcast_to(second, (TILE, count)),
                jnp.zeros((LANES - 2 * TILE, count), F32),
            ],
            axis=0,
        )
        target[...] = stacked.T

    coefficients(row_i, got_i, i_copies, coef_i)

    @pl.loop(0, rows // STRIP)
    def _(j):
        strip = pl.ds(pl.multiple_of(j * STRIP, STRIP), STRIP)
        image = img_v[strip, :].astype(F32)
        inverse = coef_i[strip, 0:1]
        second = coef_i[strip, TILE : TILE + 1]
        d_img_v[strip, :] = (inverse * (grad_strip(j) - image * second)).astype(BF16)
        n_img[pl.ds(2 * j, 2)] = (image * inverse * gains).reshape(2, TILE, cols).astype(BF16)

    @pl.loop(0, slots)
    def _(q):
        send_n[q] = n_img[maps[at_tile + q]]

    @pl.loop(0, capacity)
    def _(k):
        recv_n[grp * capacity + k] = n_img[maps[at_tile + grp * capacity + k]]

    n_copies = to_group(send_n, recv_n, n_s, n_r)
    for copy in n_copies:
        copy.start()

    plan = halving_plan(lanes)

    def block_of(rel):
        block = tp
        for bit, step in enumerate(bit_steps):
            if (rel >> bit) & 1:
                block = block + step
        return block

    def product(rel, add):
        block = block_of(rel)

        @pl.loop(0, cols // piece)
        def _(n):
            span = pl.ds(pl.multiple_of(n * piece, LANES), piece)
            value = lax.dot_general(
                d_img_v[...], w_v[block, span, :], (((1,), (1,)), ((), ())),
                preferred_element_type=F32,
            )
            if add is not None:
                value = value + first[add, :, span].astype(F32)
            part[rel, :, span] = value.astype(BF16)

    def first_copy(rel):
        return pltpu.make_async_remote_copy(
            src_ref=part.at[rel],
            dst_ref=first.at[rel // 2],
            send_sem=f_s.at[rel // 2],
            recv_sem=f_r.at[rel // 2],
            device_id={"tp": tp + bit_steps[0]},
            device_id_type=MESH,
        )

    def later_copy(side, bit, rel, number):
        return pltpu.make_async_remote_copy(
            src_ref=part.at[rel, pl.ds(side * half, half), :],
            dst_ref=later.at[side, number],
            send_sem=l_s.at[side, number],
            recv_sem=l_r.at[side, number],
            device_id={"tp": tp + bit_steps[bit]},
            device_id_type=MESH,
        )

    urgent = sorted(range(0, lanes, 2), key=lambda rel: (-bin(rel).count("1"), -rel))
    first_copies = {}
    later_copies = {}
    def send_on(side, stage, rel):
        if stage < len(plan[side]) and rel in plan[side][stage][1]:
            bit, numbers = plan[side][stage]
            copy = later_copy(side, bit, rel, numbers[rel])
            later_copies[side, numbers[rel]] = copy
            copy.start()

    def send_first(rel):
        product(rel + 1, None)
        first_copies[rel] = first_copy(rel + 1)
        first_copies[rel].start()

    send_first(urgent[0])
    for place, rel in enumerate(urgent):
        if place + 1 < len(urgent):
            send_first(urgent[place + 1])
        first_copies[rel].wait_recv()
        product(rel, rel // 2)
        for side in range(2):
            send_on(side, 0, rel)

    coefficients(row_x, got_x, x_copies, coef_x)

    @pl.loop(0, spread // 2)
    def _(j):
        strip = pl.ds(pl.multiple_of(j * STRIP, STRIP), STRIP)
        values = doc_strip(text_v, j)
        grads = doc_strip(dn_v, j) * gains
        inverse = coef_x[strip, 0:1]
        second = coef_x[strip, TILE : TILE + 1]
        normed_v[pl.ds(2 * j, 2)] = (
            (values * inverse * gains).reshape(2, TILE, cols).astype(BF16)
        )
        d_values = inverse * (grads - values * second)
        for side in range(2):
            flag = jnp.full((TILE, cols), maps[at_place + 2 * j + side], jnp.int32)
            d_text_v[2 * j + side] = jnp.where(
                flag >= 0, 0.0, d_values[side * TILE : (side + 1) * TILE, :]
            ).astype(BF16)

    @pl.loop(0, rows // STRIP)
    def _(j):
        strip = pl.ds(pl.multiple_of(j * STRIP, STRIP), STRIP)
        acc_v[strip, :] = gelu_slope(hid_v[tp // 2, strip, :].astype(F32))

    def collect(stage, last):
        for side in range(2):
            if stage >= len(plan[side]):
                continue
            bit, numbers = plan[side][stage]
            ahead = plan[side][stage + 1][1] if stage + 1 < len(plan[side]) else {}
            goal = sorted(numbers, key=lambda rel: (rel - (1 << bit)) not in ahead)
            for rel in goal:
                number = numbers[rel]
                mine = rel - (1 << bit)
                later_copies[side, number].wait_recv()
                if mine:

                    @pl.loop(0, half // STRIP)
                    def _(j):
                        here = pl.multiple_of(j * STRIP, STRIP)
                        there = pl.ds(side * half + here, STRIP)
                        part[mine, there, :] = (
                            part[mine, there, :].astype(F32)
                            + later[side, number, pl.ds(here, STRIP), :].astype(F32)
                        ).astype(BF16)

                    send_on(side, stage + 1, mine)

    stages = len(plan[0])
    for stage in range(stages - 1):
        collect(stage, False)

    for copy in n_copies:
        copy.wait_recv()

    @pl.loop(0, spread)
    def _(p):
        slot = maps[at_place + p]
        flag = jnp.full((TILE, cols), slot, jnp.int32)
        normed_v[p] = jnp.where(
            flag >= 0, recv_n[jnp.maximum(slot, 0)].astype(F32), normed_v[p].astype(F32)
        ).astype(BF16)

    if stages:
        collect(stages - 1, True)

    for side in range(2):
        tails = [numbers[1 << bit] for bit, numbers in plan[side]]

        @pl.loop(0, half // STRIP)
        def _(j):
            here = pl.multiple_of(j * STRIP, STRIP)
            there = pl.ds(side * half + here, STRIP)
            total = part[0, there, :].astype(F32)
            for number in tails:
                total = total + later[side, number, pl.ds(here, STRIP), :].astype(F32)
            d_hid_v[there, :] = (total * acc_v[there, :]).astype(BF16)

    for copy in act_copies + dn_copies + x_copies + i_copies + n_copies:
        copy.wait_send()
    for copy in list(first_copies.values()) + list(later_copies.values()):
        copy.wait_send()


def on_device(hidden, proj_weight, proj_bias, tile_pos, text_embed, norm_gain, d_normed):
    rows, width = hidden.shape
    cols = proj_weight.shape[1]
    tokens = text_embed.shape[0]
    groups = lax.axis_size("grp")
    lanes = lax.axis_size("tp")
    assert lanes >= 2 and lanes & (lanes - 1) == 0, lanes
    tiles_dev = rows // TILE
    spread = tokens // TILE
    capacity = max(2, (tiles_dev + groups - 1) // groups)
    slots = groups * capacity
    maps = tile_maps(tile_pos, groups, tiles_dev, spread, capacity)
    any_spec = pl.BlockSpec(memory_space=pl.ANY)
    vmem_spec = pl.BlockSpec(memory_space=pltpu.VMEM)
    half = rows // 2
    kept = max(1, lanes // 2 - 1)

    def vmem(*shape, dtype=BF16):
        return pltpu.VMEM(shape, dtype)

    def sems(*shape):
        return pltpu.SemaphoreType.DMA(shape)

    tiled = (spread, TILE, cols)
    normed, d_text, d_hidden = pl.pallas_call(
        functools.partial(kernel, groups, lanes, capacity),
        out_shape=(
            vmem(*tiled),
            vmem(*tiled),
            vmem(rows, cols),
        ),
        in_specs=[
            pl.BlockSpec(memory_space=pltpu.SMEM),
            any_spec, any_spec, vmem_spec, vmem_spec, any_spec, any_spec,
        ],
        out_specs=(vmem_spec, vmem_spec, vmem_spec),
        scratch_shapes=[
            vmem(lanes // 2, rows, cols),
            vmem(lanes, cols, cols),
            vmem(lanes // 2, rows, cols),
            vmem(lanes // 2, rows, cols),
            vmem(rows, cols, dtype=F32),
            vmem(rows, cols),
            vmem(rows, cols),
            vmem(*tiled),
            vmem(*tiled),
            vmem(slots, TILE, cols),
            vmem(slots, TILE, cols),
            vmem(tiles_dev, TILE, cols),
            vmem(slots, TILE, cols),
            vmem(slots, TILE, cols),
            vmem(rows, LANES, dtype=F32),
            vmem(tokens, LANES, dtype=F32),
            vmem(TILE, rows, dtype=F32),
            vmem(TILE, tokens, dtype=F32),
            vmem(lanes - 1, TILE, rows, dtype=F32),
            vmem(lanes - 1, TILE, tokens, dtype=F32),
            vmem(rows, LANES, dtype=F32),
            vmem(tokens, LANES, dtype=F32),
            vmem(lanes, rows, cols),
            vmem(lanes // 2, rows, cols),
            vmem(2, kept, half, cols),
            sems(2), sems(lanes // 2), sems(lanes), sems(lanes // 2), sems(lanes // 2),
            sems(groups - 1), sems(groups - 1), sems(groups - 1), sems(groups - 1),
            sems(lanes - 1), sems(lanes - 1), sems(lanes - 1), sems(lanes - 1),
            sems(lanes // 2), sems(lanes // 2), sems(2, kept), sems(2, kept),
        ],
        compiler_params=pltpu.CompilerParams(
            collective_id=0, has_side_effects=True, vmem_limit_bytes=58 * 1024 * 1024
        ),
        cost_estimate=pl.CostEstimate(
            flops=4 * rows * width * cols,
            bytes_accessed=2 * (width * cols + rows * width + 5 * tokens * cols),
            transcendentals=rows * width // 2,
        ),
        name="projector_norm",
    )(
        maps, hidden, proj_weight, proj_bias.reshape(1, cols), norm_gain.reshape(1, cols),
        text_embed.reshape(tiled), d_normed.reshape(tiled),
    )
    return (normed.reshape(tokens, cols), d_text.reshape(tokens, cols), d_hidden)


def solution(mesh):
    in_specs = (
        P("grp", None),
        P(None, "tp"),
        P("tp"),
        P(),
        P("grp", "tp"),
        P("tp"),
        P("grp", "tp"),
    )
    out_specs = (P("grp", "tp"), P("grp", "tp"), P("grp", "tp"))
    return jax.shard_map(
        on_device, mesh=mesh, in_specs=in_specs, out_specs=out_specs, check_vma=False
    )
```

```python
import functools

import jax
import jax.numpy as jnp
from jax import lax
from jax.experimental import pallas as pl
from jax.experimental.pallas import tpu as pltpu
from jax.sharding import PartitionSpec as P

TILE = 8
STRIP = 2 * TILE
LANES = 128
MESH = pl.DeviceIdType.MESH
F32 = jnp.float32
BF16 = jnp.bfloat16

epsilon = 1e-05


def normal_cdf(values):
    return 0.5 * (1.0 + lax.erf(values * 0.7071067811865476))


def gelu_slope(values):
    density = jnp.exp(-0.5 * values * values) * 0.3989422804014327
    return normal_cdf(values) + values * density


def tile_maps(tile_pos, groups, tiles_dev, spread, capacity):
    group_index = lax.axis_index("grp")
    slots = groups * capacity
    tile_index = jnp.arange(tile_pos.shape[0], dtype=jnp.int32)
    source = tile_index // tiles_dev
    target = lax.div(tile_pos, jnp.int32(spread))
    local_pos = tile_pos - group_index * spread
    earlier = (
        (source[:, None] == source[None, :])
        & (target[:, None] == target[None, :])
        & (tile_index[None, :] < tile_index[:, None])
    )
    standing = jnp.sum(earlier.astype(jnp.int32), axis=1)
    arrive = source * capacity + standing
    here = target == group_index
    slot_index = jnp.arange(slots, dtype=jnp.int32)
    needed = jnp.sum(
        jnp.where(here[None, :] & (arrive[None, :] == slot_index[:, None]), local_pos[None, :], 0),
        axis=1,
    )
    depart = target * capacity + standing
    mine = source == group_index
    own_slot = lax.dynamic_slice_in_dim(depart, group_index * tiles_dev, tiles_dev, 0)
    tile_of_slot = jnp.sum(
        jnp.where(
            mine[None, :] & (depart[None, :] == slot_index[:, None]),
            (tile_index - group_index * tiles_dev)[None, :],
            0,
        ),
        axis=1,
    )
    hits = local_pos[None, :] == jnp.arange(spread, dtype=jnp.int32)[:, None]
    place = jnp.sum(jnp.where(hits, arrive[None, :] + 1, 0), axis=1) - 1
    return jnp.concatenate([needed, own_slot, tile_of_slot, place])


def halving_plan(lanes):
    bits = lanes.bit_length() - 1
    orders = (list(range(1, bits)), list(range(bits - 1, 0, -1)))
    plan = []
    for order in orders:
        kept = [rel for rel in range(lanes) if rel % 2 == 0]
        stages = []
        number = 0
        for bit in order:
            sent = [rel for rel in kept if (rel >> bit) & 1]
            kept = [rel for rel in kept if not (rel >> bit) & 1]
            stages.append((bit, {rel: number + place for place, rel in enumerate(sent)}))
            number += len(sent)
        plan.append(stages)
    return plan


def kernel(
    groups, lanes, capacity,
    maps, hidden, weight, bias, gain, text, d_normed,
    normed_v, d_text_v, d_hid_v,
    hid_v, w_v, act_v, act_got, acc_v, img_v, d_img_v, text_v, dn_v,
    send_dn, recv_dn, n_img, send_n, recv_n,
    stat_i, stat_x, row_i, row_x, got_i, got_x, coef_i, coef_x,
    part, first, later,
    load_sem, hid_sem, w_sem, a_s, a_r,
    dn_s, dn_r, n_s, n_r, si_s, si_r, sx_s, sx_r, f_s, f_r, l_s, l_r,
):
    grp = lax.axis_index("grp")
    tp = lax.axis_index("tp")
    rows, cols = img_v.shape
    spread = text_v.shape[0]
    tiles_dev = rows // TILE
    slots = groups * capacity
    width = cols * lanes
    half = rows // 2
    piece = cols // 2 if cols % (2 * LANES) == 0 else cols
    at_slot, at_tile, at_place = slots, slots + tiles_dev, 2 * slots + tiles_dev

    odd = tp % 2
    pairs = lanes // 2

    def hid_copy(k):
        return pltpu.make_async_copy(
            hidden.at[:, pl.ds(pl.multiple_of((2 * k + odd) * cols, cols), cols)],
            hid_v.at[k],
            hid_sem.at[k],
        )

    def w_copy(k, other):
        block = 2 * k + (1 - odd if other else odd)
        return pltpu.make_async_copy(
            weight.at[pl.ds(pl.multiple_of(block * cols, cols), cols), :],
            w_v.at[block],
            w_sem.at[2 * k + other],
        )

    dn_copy = pltpu.make_async_copy(d_normed, dn_v, load_sem.at[0])
    text_copy = pltpu.make_async_copy(text, text_v, load_sem.at[1])
    dn_copy.start()
    hid_copy(0).start()
    w_copy(0, 0).start()
    for k in range(1, pairs):
        hid_copy(k).start()
        w_copy(k, 0).start()
        w_copy(k - 1, 1).start()
    w_copy(pairs - 1, 1).start()
    text_copy.start()

    barrier = pltpu.get_barrier_semaphore()
    for d in range(1, groups):
        pl.semaphore_signal(
            barrier, inc=1, device_id={"grp": (grp + d) % groups}, device_id_type=MESH
        )
    for d in range(1, lanes):
        pl.semaphore_signal(
            barrier, inc=1, device_id={"tp": (tp + d) % lanes}, device_id_type=MESH
        )

    def to_group(source, target, send, receive):
        copies = []
        for d in sorted(range(1, groups), key=lambda d: abs(2 * d - groups)):
            peer = (grp + d) % groups
            copies.append(
                pltpu.make_async_remote_copy(
                    src_ref=source.at[pl.ds(peer * capacity, capacity)],
                    dst_ref=target.at[pl.ds(grp * capacity, capacity)],
                    send_sem=send.at[d - 1],
                    recv_sem=receive.at[d - 1],
                    device_id={"grp": peer},
                    device_id_type=MESH,
                )
            )
        return copies

    def to_lanes(source, target, send, receive):
        return [
            pltpu.make_async_remote_copy(
                src_ref=source,
                dst_ref=target.at[d - 1],
                send_sem=send.at[d - 1],
                recv_sem=receive.at[d - 1],
                device_id={"tp": (tp + d) % lanes},
                device_id_type=MESH,
            )
            for d in range(1, lanes)
        ]

    dn_copy.wait()

    @pl.loop(0, slots)
    def _(q):
        send_dn[q] = dn_v[maps[q]]

    @pl.loop(0, capacity)
    def _(k):
        recv_dn[grp * capacity + k] = dn_v[maps[grp * capacity + k]]

    pl.semaphore_wait(barrier, groups + lanes - 2)
    dn_copies = to_group(send_dn, recv_dn, dn_s, dn_r)
    for copy in dn_copies:
        copy.start()

    gains = gain[...]
    lane = lax.broadcasted_iota(jnp.int32, (STRIP, LANES), 1)

    def row_sums(values, grads):
        squares = jnp.sum(values * values, axis=1, keepdims=True)
        crosses = jnp.sum(grads * values, axis=1, keepdims=True)
        return jnp.where(lane == 0, squares, jnp.where(lane == 1, crosses, 0.0))

    def doc_strip(ref, j):
        return ref[pl.ds(2 * j, 2)].astype(F32).reshape(STRIP, cols)

    bit_steps = []
    left = tp
    for bit in range(lanes.bit_length() - 1):
        bit_steps.append((1 - 2 * (left % 2)) * (1 << bit))
        left = left // 2

    act_copies = [
        pltpu.make_async_remote_copy(
            src_ref=act_v.at[k],
            dst_ref=act_got.at[k],
            send_sem=a_s.at[k],
            recv_sem=a_r.at[k],
            device_id={"tp": tp + bit_steps[0]},
            device_id_type=MESH,
        )
        for k in range(pairs)
    ]
    steps = min(4, cols // LANES)
    span_width = cols // steps
    strips = rows // STRIP // steps

    def forward(k, ready):
        if k is not None:
            hid_copy(k).wait()
        for source, other in ready:
            w_copy(source, other).wait()
            if other:
                act_copies[source].wait_recv()

        @pl.loop(0, steps)
        def _(n):
            if k is not None:
                for j in range(strips):
                    strip = pl.ds(pl.multiple_of((n * strips + j) * STRIP, STRIP), STRIP)
                    values = hid_v[k, strip, :].astype(F32)
                    act_v[k, strip, :] = (values * normal_cdf(values)).astype(BF16)
            if ready:
                span = pl.ds(pl.multiple_of(n * span_width, LANES), span_width)
                total = None if ready[0] == (0, 0) else acc_v[:, span]
                for source, other in ready:
                    block = 2 * source + (1 - odd if other else odd)
                    left_side = act_got[source] if other else act_v[source]
                    value = jnp.dot(
                        left_side, w_v[block, :, span], preferred_element_type=F32
                    )
                    total = value if total is None else total + value
                acc_v[:, span] = total

        if k is not None:
            act_copies[k].start()

    for k in range(pairs):
        ready = []
        if k >= 1:
            ready.append((k - 1, 0))
        if k >= 2:
            ready.append((k - 2, 1))
        forward(k, ready)
    tail = [(pairs - 1, 0)]
    if pairs >= 2:
        tail.append((pairs - 2, 1))
    forward(None, tail)
    forward(None, [(pairs - 1, 1)])

    for copy in dn_copies:
        copy.wait_recv()

    def grad_strip(j):
        one = recv_dn[maps[at_slot + 2 * j]].astype(F32)
        two = recv_dn[maps[at_slot + 2 * j + 1]].astype(F32)
        return jnp.concatenate([one, two], axis=0) * gains

    biases = bias[...]

    @pl.loop(0, rows // STRIP)
    def _(j):
        strip = pl.ds(pl.multiple_of(j * STRIP, STRIP), STRIP)
        image = (acc_v[strip, :] + biases).astype(BF16)
        img_v[strip, :] = image
        stat_i[strip, :] = row_sums(image.astype(F32), grad_strip(j))

    row_i[...] = stat_i[...].T[:TILE, :]
    i_copies = to_lanes(row_i, got_i, si_s, si_r)
    for copy in i_copies:
        copy.start()

    text_copy.wait()

    @pl.loop(0, spread // 2)
    def _(j):
        grads = doc_strip(dn_v, j) * gains
        stat_x[pl.ds(pl.multiple_of(j * STRIP, STRIP), STRIP), :] = row_sums(
            doc_strip(text_v, j), grads
        )

    row_x[...] = stat_x[...].T[:TILE, :]
    x_copies = to_lanes(row_x, got_x, sx_s, sx_r)
    for copy in x_copies:
        copy.start()

    def coefficients(own, got, copies, target):
        for copy in copies:
            copy.wait_recv()
        total = own[...]
        for d in range(lanes - 1):
            total = total + got[d]
        inverse = lax.rsqrt(total[0:1, :] / width + epsilon)
        second = inverse * inverse * (total[1:2, :] / width)
        count = own.shape[1]
        stacked = jnp.concatenate(
            [
                jnp.broadcast_to(inverse, (TILE, count)),
                jnp.broadcast_to(second, (TILE, count)),
                jnp.zeros((LANES - 2 * TILE, count), F32),
            ],
            axis=0,
        )
        target[...] = stacked.T

    coefficients(row_i, got_i, i_copies, coef_i)

    @pl.loop(0, rows // STRIP)
    def _(j):
        strip = pl.ds(pl.multiple_of(j * STRIP, STRIP), STRIP)
        image = img_v[strip, :].astype(F32)
        inverse = coef_i[strip, 0:1]
        second = coef_i[strip, TILE : TILE + 1]
        d_img_v[strip, :] = (inverse * (grad_strip(j) - image * second)).astype(BF16)

    plan = halving_plan(lanes)

    def block_of(rel):
        block = tp
        for bit, step in enumerate(bit_steps):
            if (rel >> bit) & 1:
                block = block + step
        return block

    def product(rel, add):
        block = block_of(rel)

        @pl.loop(0, cols // piece)
        def _(n):
            span = pl.ds(pl.multiple_of(n * piece, LANES), piece)
            value = lax.dot_general(
                d_img_v[...], w_v[block, span, :], (((1,), (1,)), ((), ())),
                preferred_element_type=F32,
            )
            if add is not None:
                value = value + first[add, :, span].astype(F32)
            part[rel, :, span] = value.astype(BF16)

    def first_copy(rel):
        return pltpu.make_async_remote_copy(
            src_ref=part.at[rel],
            dst_ref=first.at[rel // 2],
            send_sem=f_s.at[rel // 2],
            recv_sem=f_r.at[rel // 2],
            device_id={"tp": tp + bit_steps[0]},
            device_id_type=MESH,
        )

    def later_copy(side, bit, rel, number):
        return pltpu.make_async_remote_copy(
            src_ref=part.at[rel, pl.ds(side * half, half), :],
            dst_ref=later.at[side, number],
            send_sem=l_s.at[side, number],
            recv_sem=l_r.at[side, number],
            device_id={"tp": tp + bit_steps[bit]},
            device_id_type=MESH,
        )

    urgent = sorted(range(0, lanes, 2), key=lambda rel: (-bin(rel).count("1"), -rel))
    first_copies = {}
    later_copies = {}
    def send_on(side, stage, rel):
        if stage < len(plan[side]) and rel in plan[side][stage][1]:
            bit, numbers = plan[side][stage]
            copy = later_copy(side, bit, rel, numbers[rel])
            later_copies[side, numbers[rel]] = copy
            copy.start()

    def send_first(rel):
        product(rel + 1, None)
        first_copies[rel] = first_copy(rel + 1)
        first_copies[rel].start()

    def normed_tiles():
        @pl.loop(0, rows // STRIP)
        def _(j):
            strip = pl.ds(pl.multiple_of(j * STRIP, STRIP), STRIP)
            image = img_v[strip, :].astype(F32)
            inverse = coef_i[strip, 0:1]
            n_img[pl.ds(2 * j, 2)] = (
                (image * inverse * gains).reshape(2, TILE, cols).astype(BF16)
            )

        @pl.loop(0, slots)
        def _(q):
            send_n[q] = n_img[maps[at_tile + q]]

        @pl.loop(0, capacity)
        def _(k):
            recv_n[grp * capacity + k] = n_img[maps[at_tile + grp * capacity + k]]

        copies = to_group(send_n, recv_n, n_s, n_r)
        for copy in copies:
            copy.start()
        return copies

    send_first(urgent[0])
    for place, rel in enumerate(urgent):
        if place + 1 < len(urgent):
            send_first(urgent[place + 1])
        first_copies[rel].wait_recv()
        product(rel, rel // 2)
        for side in range(2):
            send_on(side, 0, rel)
        if place == 0:
            n_copies = normed_tiles()

    coefficients(row_x, got_x, x_copies, coef_x)

    @pl.loop(0, spread // 2)
    def _(j):
        strip = pl.ds(pl.multiple_of(j * STRIP, STRIP), STRIP)
        values = doc_strip(text_v, j)
        grads = doc_strip(dn_v, j) * gains
        inverse = coef_x[strip, 0:1]
        second = coef_x[strip, TILE : TILE + 1]
        normed_v[pl.ds(2 * j, 2)] = (
            (values * inverse * gains).reshape(2, TILE, cols).astype(BF16)
        )
        d_values = inverse * (grads - values * second)
        for side in range(2):
            flag = jnp.full((TILE, cols), maps[at_place + 2 * j + side], jnp.int32)
            d_text_v[2 * j + side] = jnp.where(
                flag >= 0, 0.0, d_values[side * TILE : (side + 1) * TILE, :]
            ).astype(BF16)

    @pl.loop(0, rows // STRIP)
    def _(j):
        strip = pl.ds(pl.multiple_of(j * STRIP, STRIP), STRIP)
        acc_v[strip, :] = gelu_slope(hid_v[tp // 2, strip, :].astype(F32))

    def collect(stage, last):
        for side in range(2):
            if stage >= len(plan[side]):
                continue
            bit, numbers = plan[side][stage]
            ahead = plan[side][stage + 1][1] if stage + 1 < len(plan[side]) else {}
            goal = sorted(numbers, key=lambda rel: (rel - (1 << bit)) not in ahead)
            for rel in goal:
                number = numbers[rel]
                mine = rel - (1 << bit)
                later_copies[side, number].wait_recv()
                if mine:

                    @pl.loop(0, half // STRIP)
                    def _(j):
                        here = pl.multiple_of(j * STRIP, STRIP)
                        there = pl.ds(side * half + here, STRIP)
                        part[mine, there, :] = (
                            part[mine, there, :].astype(F32)
                            + later[side, number, pl.ds(here, STRIP), :].astype(F32)
                        ).astype(BF16)

                    send_on(side, stage + 1, mine)

    stages = len(plan[0])
    for stage in range(stages - 1):
        collect(stage, False)

    for copy in n_copies:
        copy.wait_recv()

    @pl.loop(0, spread)
    def _(p):
        slot = maps[at_place + p]
        flag = jnp.full((TILE, cols), slot, jnp.int32)
        normed_v[p] = jnp.where(
            flag >= 0, recv_n[jnp.maximum(slot, 0)].astype(F32), normed_v[p].astype(F32)
        ).astype(BF16)

    if stages:
        collect(stages - 1, True)

    for side in range(2):
        tails = [numbers[1 << bit] for bit, numbers in plan[side]]

        @pl.loop(0, half // STRIP)
        def _(j):
            here = pl.multiple_of(j * STRIP, STRIP)
            there = pl.ds(side * half + here, STRIP)
            total = part[0, there, :].astype(F32)
            for number in tails:
                total = total + later[side, number, pl.ds(here, STRIP), :].astype(F32)
            d_hid_v[there, :] = (total * acc_v[there, :]).astype(BF16)

    for copy in act_copies + dn_copies + x_copies + i_copies + n_copies:
        copy.wait_send()
    for copy in list(first_copies.values()) + list(later_copies.values()):
        copy.wait_send()


def hand_out(*refs):
    count = len(refs) // 2
    sem = refs[-1]
    copies = []
    for number in range(count):
        source, target = refs[number], refs[count + number]
        cut = source.shape[0] // 2
        for side in range(2):
            span = pl.ds(side * cut, cut)
            copies.append(
                pltpu.make_async_copy(
                    source.at[span], target.at[span], sem.at[2 * number + side]
                )
            )
    for copy in copies:
        copy.start()
    for copy in copies:
        copy.wait()


def on_device(hidden, proj_weight, proj_bias, tile_pos, text_embed, norm_gain, d_normed):
    rows, width = hidden.shape
    cols = proj_weight.shape[1]
    tokens = text_embed.shape[0]
    groups = lax.axis_size("grp")
    lanes = lax.axis_size("tp")
    assert lanes >= 2 and lanes & (lanes - 1) == 0, lanes
    tiles_dev = rows // TILE
    spread = tokens // TILE
    capacity = max(2, (tiles_dev + groups - 1) // groups)
    slots = groups * capacity
    maps = tile_maps(tile_pos, groups, tiles_dev, spread, capacity)
    any_spec = pl.BlockSpec(memory_space=pl.ANY)
    vmem_spec = pl.BlockSpec(memory_space=pltpu.VMEM)
    half = rows // 2
    kept = max(1, lanes // 2 - 1)

    def vmem(*shape, dtype=BF16):
        return pltpu.VMEM(shape, dtype)

    def sems(*shape):
        return pltpu.SemaphoreType.DMA(shape)

    tiled = (spread, TILE, cols)
    normed, d_text, d_hidden = pl.pallas_call(
        functools.partial(kernel, groups, lanes, capacity),
        out_shape=(
            vmem(*tiled),
            vmem(*tiled),
            vmem(rows, cols),
        ),
        in_specs=[
            pl.BlockSpec(memory_space=pltpu.SMEM),
            any_spec, any_spec, vmem_spec, vmem_spec, any_spec, any_spec,
        ],
        out_specs=(vmem_spec, vmem_spec, vmem_spec),
        scratch_shapes=[
            vmem(lanes // 2, rows, cols),
            vmem(lanes, cols, cols),
            vmem(lanes // 2, rows, cols),
            vmem(lanes // 2, rows, cols),
            vmem(rows, cols, dtype=F32),
            vmem(rows, cols),
            vmem(rows, cols),
            vmem(*tiled),
            vmem(*tiled),
            vmem(slots, TILE, cols),
            vmem(slots, TILE, cols),
            vmem(tiles_dev, TILE, cols),
            vmem(slots, TILE, cols),
            vmem(slots, TILE, cols),
            vmem(rows, LANES, dtype=F32),
            vmem(tokens, LANES, dtype=F32),
            vmem(TILE, rows, dtype=F32),
            vmem(TILE, tokens, dtype=F32),
            vmem(lanes - 1, TILE, rows, dtype=F32),
            vmem(lanes - 1, TILE, tokens, dtype=F32),
            vmem(rows, LANES, dtype=F32),
            vmem(tokens, LANES, dtype=F32),
            vmem(lanes, rows, cols),
            vmem(lanes // 2, rows, cols),
            vmem(2, kept, half, cols),
            sems(2), sems(lanes // 2), sems(lanes), sems(lanes // 2), sems(lanes // 2),
            sems(groups - 1), sems(groups - 1), sems(groups - 1), sems(groups - 1),
            sems(lanes - 1), sems(lanes - 1), sems(lanes - 1), sems(lanes - 1),
            sems(lanes // 2), sems(lanes // 2), sems(2, kept), sems(2, kept),
        ],
        compiler_params=pltpu.CompilerParams(
            collective_id=0, has_side_effects=True, vmem_limit_bytes=58 * 1024 * 1024
        ),
        cost_estimate=pl.CostEstimate(
            flops=4 * rows * width * cols,
            bytes_accessed=2 * (width * cols + rows * width + 5 * tokens * cols),
            transcendentals=rows * width // 2,
        ),
        name="projector_norm",
    )(
        maps, hidden, proj_weight, proj_bias.reshape(1, cols), norm_gain.reshape(1, cols),
        text_embed.reshape(tiled), d_normed.reshape(tiled),
    )
    normed, d_text, d_hidden = pl.pallas_call(
        hand_out,
        out_shape=(
            jax.ShapeDtypeStruct(tiled, BF16),
            jax.ShapeDtypeStruct(tiled, BF16),
            jax.ShapeDtypeStruct((rows, cols), BF16),
        ),
        in_specs=[any_spec] * 3,
        out_specs=(any_spec,) * 3,
        scratch_shapes=[sems(6)],
        compiler_params=pltpu.CompilerParams(vmem_limit_bytes=1024 * 1024),
        name="hand_out",
    )(normed, d_text, d_hidden)
    return (normed.reshape(tokens, cols), d_text.reshape(tokens, cols), d_hidden)


def solution(mesh):
    in_specs = (
        P("grp", None),
        P(None, "tp"),
        P("tp"),
        P(),
        P("grp", "tp"),
        P("tp"),
        P("grp", "tp"),
    )
    out_specs = (P("grp", "tp"), P("grp", "tp"), P("grp", "tp"))
    return jax.shard_map(
        on_device, mesh=mesh, in_specs=in_specs, out_specs=out_specs, check_vma=False
    )
```

```python
import functools

import jax
import jax.numpy as jnp
from jax import lax
from jax.experimental import pallas as pl
from jax.experimental.pallas import tpu as pltpu
from jax.sharding import PartitionSpec as P

TILE = 8
STRIP = 2 * TILE
LANES = 128
MESH = pl.DeviceIdType.MESH
F32 = jnp.float32
BF16 = jnp.bfloat16

epsilon = 1e-05


def normal_cdf(values):
    return 0.5 * (1.0 + lax.erf(values * 0.7071067811865476))


def gelu_slope(values):
    density = jnp.exp(-0.5 * values * values) * 0.3989422804014327
    return normal_cdf(values) + values * density


def tile_maps(tile_pos, groups, tiles_dev, spread, capacity):
    group_index = lax.axis_index("grp")
    slots = groups * capacity
    tile_index = jnp.arange(tile_pos.shape[0], dtype=jnp.int32)
    source = tile_index // tiles_dev
    local_pos = lax.optimization_barrier(tile_pos - group_index * spread)
    target = lax.div(local_pos + group_index * spread, jnp.int32(spread))
    earlier = (
        (source[:, None] == source[None, :])
        & (target[:, None] == target[None, :])
        & (tile_index[None, :] < tile_index[:, None])
    )
    standing = jnp.sum(earlier.astype(jnp.int32), axis=1)
    arrive = source * capacity + standing
    here = target == group_index
    slot_index = jnp.arange(slots, dtype=jnp.int32)
    needed = jnp.sum(
        jnp.where(here[None, :] & (arrive[None, :] == slot_index[:, None]), local_pos[None, :], 0),
        axis=1,
    )
    depart = target * capacity + standing
    mine = source == group_index
    own_slot = lax.dynamic_slice_in_dim(depart, group_index * tiles_dev, tiles_dev, 0)
    tile_of_slot = jnp.sum(
        jnp.where(
            mine[None, :] & (depart[None, :] == slot_index[:, None]),
            (tile_index - group_index * tiles_dev)[None, :],
            0,
        ),
        axis=1,
    )
    hits = local_pos[None, :] == jnp.arange(spread, dtype=jnp.int32)[:, None]
    place = jnp.sum(jnp.where(hits, arrive[None, :] + 1, 0), axis=1) - 1
    return jnp.concatenate([needed, own_slot, tile_of_slot, place])


def halving_plan(lanes):
    bits = lanes.bit_length() - 1
    orders = (list(range(1, bits)), list(range(bits - 1, 0, -1)))
    plan = []
    for order in orders:
        kept = [rel for rel in range(lanes) if rel % 2 == 0]
        stages = []
        number = 0
        for bit in order:
            sent = [rel for rel in kept if (rel >> bit) & 1]
            kept = [rel for rel in kept if not (rel >> bit) & 1]
            stages.append((bit, {rel: number + place for place, rel in enumerate(sent)}))
            number += len(sent)
        plan.append(stages)
    return plan


def kernel(
    groups, lanes, capacity,
    maps, hidden, weight, bias, gain, text, d_normed,
    normed_v, d_text_v, d_hid_v,
    hid_v, w_v, act_v, act_got, acc_v, img_v, d_img_v, text_v, dn_v,
    send_dn, recv_dn, n_img, send_n, recv_n,
    stat_i, stat_x, row_i, row_x, got_i, got_x, coef_i, coef_x,
    part, first, later,
    load_sem, hid_sem, w_sem, a_s, a_r,
    dn_s, dn_r, n_s, n_r, si_s, si_r, sx_s, sx_r, f_s, f_r, l_s, l_r,
):
    grp = lax.axis_index("grp")
    tp = lax.axis_index("tp")
    rows, cols = img_v.shape
    spread = text_v.shape[0]
    tiles_dev = rows // TILE
    slots = groups * capacity
    width = cols * lanes
    half = rows // 2
    piece = cols // 2 if cols % (2 * LANES) == 0 else cols
    at_slot, at_tile, at_place = slots, slots + tiles_dev, 2 * slots + tiles_dev

    odd = tp % 2
    pairs = lanes // 2

    def hid_copy(k):
        return pltpu.make_async_copy(
            hidden.at[:, pl.ds(pl.multiple_of((2 * k + odd) * cols, cols), cols)],
            hid_v.at[k],
            hid_sem.at[k],
        )

    def w_copy(k, other):
        block = 2 * k + (1 - odd if other else odd)
        return pltpu.make_async_copy(
            weight.at[pl.ds(pl.multiple_of(block * cols, cols), cols), :],
            w_v.at[block],
            w_sem.at[2 * k + other],
        )

    dn_copy = pltpu.make_async_copy(d_normed, dn_v, load_sem.at[0])
    text_copy = pltpu.make_async_copy(text, text_v, load_sem.at[1])
    dn_copy.start()
    hid_copy(0).start()
    w_copy(0, 0).start()
    for k in range(1, pairs):
        hid_copy(k).start()
        w_copy(k, 0).start()
        w_copy(k - 1, 1).start()
    w_copy(pairs - 1, 1).start()
    text_copy.start()

    barrier = pltpu.get_barrier_semaphore()
    for d in range(1, groups):
        pl.semaphore_signal(
            barrier, inc=1, device_id={"grp": (grp + d) % groups}, device_id_type=MESH
        )
    for d in range(1, lanes):
        pl.semaphore_signal(
            barrier, inc=1, device_id={"tp": (tp + d) % lanes}, device_id_type=MESH
        )

    def to_group(source, target, send, receive):
        copies = []
        for d in sorted(range(1, groups), key=lambda d: abs(2 * d - groups)):
            peer = (grp + d) % groups
            copies.append(
                pltpu.make_async_remote_copy(
                    src_ref=source.at[pl.ds(peer * capacity, capacity)],
                    dst_ref=target.at[pl.ds(grp * capacity, capacity)],
                    send_sem=send.at[d - 1],
                    recv_sem=receive.at[d - 1],
                    device_id={"grp": peer},
                    device_id_type=MESH,
                )
            )
        return copies

    def to_lanes(source, target, send, receive):
        return [
            pltpu.make_async_remote_copy(
                src_ref=source,
                dst_ref=target.at[d - 1],
                send_sem=send.at[d - 1],
                recv_sem=receive.at[d - 1],
                device_id={"tp": (tp + d) % lanes},
                device_id_type=MESH,
            )
            for d in range(1, lanes)
        ]

    dn_copy.wait()

    @pl.loop(0, slots)
    def _(q):
        send_dn[q] = dn_v[maps[q]]

    pl.semaphore_wait(barrier, groups + lanes - 2)
    dn_copies = to_group(send_dn, recv_dn, dn_s, dn_r)
    for copy in dn_copies:
        copy.start()

    @pl.loop(0, capacity)
    def _(k):
        recv_dn[grp * capacity + k] = dn_v[maps[grp * capacity + k]]

    gains = gain[...]
    lane = lax.broadcasted_iota(jnp.int32, (STRIP, LANES), 1)

    def row_sums(values, grads):
        squares = jnp.sum(values * values, axis=1, keepdims=True)
        crosses = jnp.sum(grads * values, axis=1, keepdims=True)
        return jnp.where(lane == 0, squares, jnp.where(lane == 1, crosses, 0.0))

    def doc_strip(ref, j):
        return ref[pl.ds(2 * j, 2)].astype(F32).reshape(STRIP, cols)

    bit_steps = []
    left = tp
    for bit in range(lanes.bit_length() - 1):
        bit_steps.append((1 - 2 * (left % 2)) * (1 << bit))
        left = left // 2

    act_copies = [
        pltpu.make_async_remote_copy(
            src_ref=act_v.at[k],
            dst_ref=act_got.at[k],
            send_sem=a_s.at[k],
            recv_sem=a_r.at[k],
            device_id={"tp": tp + bit_steps[0]},
            device_id_type=MESH,
        )
        for k in range(pairs)
    ]
    steps = min(4, cols // LANES)
    span_width = cols // steps
    strips = rows // STRIP // steps

    def forward(k, ready):
        if k is not None:
            hid_copy(k).wait()
        for source, other in ready:
            w_copy(source, other).wait()
            if other:
                act_copies[source].wait_recv()

        @pl.loop(0, steps)
        def _(n):
            if k is not None:
                for j in range(strips):
                    strip = pl.ds(pl.multiple_of((n * strips + j) * STRIP, STRIP), STRIP)
                    values = hid_v[k, strip, :].astype(F32)
                    act_v[k, strip, :] = (values * normal_cdf(values)).astype(BF16)
            if ready:
                span = pl.ds(pl.multiple_of(n * span_width, LANES), span_width)
                total = None if ready[0] == (0, 0) else acc_v[:, span]
                for source, other in ready:
                    block = 2 * source + (1 - odd if other else odd)
                    left_side = act_got[source] if other else act_v[source]
                    value = jnp.dot(
                        left_side, w_v[block, :, span], preferred_element_type=F32
                    )
                    total = value if total is None else total + value
                acc_v[:, span] = total

        if k is not None:
            act_copies[k].start()

    for k in range(pairs):
        ready = []
        if k >= 1:
            ready.append((k - 1, 0))
        if k >= 2:
            ready.append((k - 2, 1))
        forward(k, ready)
    tail = [(pairs - 1, 0)]
    if pairs >= 2:
        tail.append((pairs - 2, 1))
    forward(None, tail)
    forward(None, [(pairs - 1, 1)])

    for copy in dn_copies:
        copy.wait_recv()

    def grad_strip(j):
        one = recv_dn[maps[at_slot + 2 * j]].astype(F32)
        two = recv_dn[maps[at_slot + 2 * j + 1]].astype(F32)
        return jnp.concatenate([one, two], axis=0) * gains

    biases = bias[...]

    @pl.loop(0, rows // STRIP)
    def _(j):
        strip = pl.ds(pl.multiple_of(j * STRIP, STRIP), STRIP)
        image = (acc_v[strip, :] + biases).astype(BF16)
        img_v[strip, :] = image
        stat_i[strip, :] = row_sums(image.astype(F32), grad_strip(j))

    row_i[...] = stat_i[...].T[:TILE, :]
    i_copies = to_lanes(row_i, got_i, si_s, si_r)
    for copy in i_copies:
        copy.start()

    text_copy.wait()

    @pl.loop(0, spread // 2)
    def _(j):
        grads = doc_strip(dn_v, j) * gains
        stat_x[pl.ds(pl.multiple_of(j * STRIP, STRIP), STRIP), :] = row_sums(
            doc_strip(text_v, j), grads
        )

    row_x[...] = stat_x[...].T[:TILE, :]
    x_copies = to_lanes(row_x, got_x, sx_s, sx_r)
    for copy in x_copies:
        copy.start()

    def coefficients(own, got, copies, target):
        for copy in copies:
            copy.wait_recv()
        total = own[...]
        for d in range(lanes - 1):
            total = total + got[d]
        inverse = lax.rsqrt(total[0:1, :] / width + epsilon)
        second = inverse * inverse * (total[1:2, :] / width)
        count = own.shape[1]
        stacked = jnp.concatenate(
            [
                jnp.broadcast_to(inverse, (TILE, count)),
                jnp.broadcast_to(second, (TILE, count)),
                jnp.zeros((LANES - 2 * TILE, count), F32),
            ],
            axis=0,
        )
        target[...] = stacked.T

    coefficients(row_i, got_i, i_copies, coef_i)

    @pl.loop(0, rows // STRIP)
    def _(j):
        strip = pl.ds(pl.multiple_of(j * STRIP, STRIP), STRIP)
        image = img_v[strip, :].astype(F32)
        inverse = coef_i[strip, 0:1]
        second = coef_i[strip, TILE : TILE + 1]
        d_img_v[strip, :] = (inverse * (grad_strip(j) - image * second)).astype(BF16)

    plan = halving_plan(lanes)

    def block_of(rel):
        block = tp
        for bit, step in enumerate(bit_steps):
            if (rel >> bit) & 1:
                block = block + step
        return block

    def product(rel, add):
        block = block_of(rel)

        @pl.loop(0, cols // piece)
        def _(n):
            span = pl.ds(pl.multiple_of(n * piece, LANES), piece)
            value = lax.dot_general(
                d_img_v[...], w_v[block, span, :], (((1,), (1,)), ((), ())),
                preferred_element_type=F32,
            )
            if add is not None:
                value = value + first[add, :, span].astype(F32)
            part[rel, :, span] = value.astype(BF16)

    def first_copy(rel):
        return pltpu.make_async_remote_copy(
            src_ref=part.at[rel],
            dst_ref=first.at[rel // 2],
            send_sem=f_s.at[rel // 2],
            recv_sem=f_r.at[rel // 2],
            device_id={"tp": tp + bit_steps[0]},
            device_id_type=MESH,
        )

    def later_copy(side, bit, rel, number):
        return pltpu.make_async_remote_copy(
            src_ref=part.at[rel, pl.ds(side * half, half), :],
            dst_ref=later.at[side, number],
            send_sem=l_s.at[side, number],
            recv_sem=l_r.at[side, number],
            device_id={"tp": tp + bit_steps[bit]},
            device_id_type=MESH,
        )

    urgent = sorted(range(0, lanes, 2), key=lambda rel: (-bin(rel).count("1"), -rel))
    first_copies = {}
    later_copies = {}
    def send_on(side, stage, rel):
        if stage < len(plan[side]) and rel in plan[side][stage][1]:
            bit, numbers = plan[side][stage]
            copy = later_copy(side, bit, rel, numbers[rel])
            later_copies[side, numbers[rel]] = copy
            copy.start()

    def send_first(rel):
        product(rel + 1, None)
        first_copies[rel] = first_copy(rel + 1)
        first_copies[rel].start()

    def normed_tiles():
        @pl.loop(0, rows // STRIP)
        def _(j):
            strip = pl.ds(pl.multiple_of(j * STRIP, STRIP), STRIP)
            image = img_v[strip, :].astype(F32)
            inverse = coef_i[strip, 0:1]
            n_img[pl.ds(2 * j, 2)] = (
                (image * inverse * gains).reshape(2, TILE, cols).astype(BF16)
            )

        @pl.loop(0, slots)
        def _(q):
            send_n[q] = n_img[maps[at_tile + q]]

        @pl.loop(0, capacity)
        def _(k):
            recv_n[grp * capacity + k] = n_img[maps[at_tile + grp * capacity + k]]

        copies = to_group(send_n, recv_n, n_s, n_r)
        for copy in copies:
            copy.start()
        return copies

    send_first(urgent[0])
    for place, rel in enumerate(urgent):
        if place + 1 < len(urgent):
            send_first(urgent[place + 1])
        first_copies[rel].wait_recv()
        product(rel, rel // 2)
        for side in range(2):
            send_on(side, 0, rel)
        if place == 0:
            n_copies = normed_tiles()

    coefficients(row_x, got_x, x_copies, coef_x)

    @pl.loop(0, spread // 2)
    def _(j):
        strip = pl.ds(pl.multiple_of(j * STRIP, STRIP), STRIP)
        values = doc_strip(text_v, j)
        grads = doc_strip(dn_v, j) * gains
        inverse = coef_x[strip, 0:1]
        second = coef_x[strip, TILE : TILE + 1]
        normed_v[pl.ds(2 * j, 2)] = (
            (values * inverse * gains).reshape(2, TILE, cols).astype(BF16)
        )
        d_values = inverse * (grads - values * second)
        for side in range(2):
            flag = jnp.full((TILE, cols), maps[at_place + 2 * j + side], jnp.int32)
            d_text_v[2 * j + side] = jnp.where(
                flag >= 0, 0.0, d_values[side * TILE : (side + 1) * TILE, :]
            ).astype(BF16)

    def collect(stage, last):
        for side in range(2):
            if stage >= len(plan[side]):
                continue
            bit, numbers = plan[side][stage]
            ahead = plan[side][stage + 1][1] if stage + 1 < len(plan[side]) else {}
            goal = sorted(numbers, key=lambda rel: (rel - (1 << bit)) not in ahead)
            for rel in goal:
                number = numbers[rel]
                mine = rel - (1 << bit)
                later_copies[side, number].wait_recv()
                if mine:

                    @pl.loop(0, half // STRIP)
                    def _(j):
                        here = pl.multiple_of(j * STRIP, STRIP)
                        there = pl.ds(side * half + here, STRIP)
                        part[mine, there, :] = (
                            part[mine, there, :].astype(F32)
                            + later[side, number, pl.ds(here, STRIP), :].astype(F32)
                        ).astype(BF16)

                    send_on(side, stage + 1, mine)

    stages = len(plan[0])
    for stage in range(stages - 1):
        collect(stage, False)

    @pl.loop(0, rows // STRIP)
    def _(j):
        strip = pl.ds(pl.multiple_of(j * STRIP, STRIP), STRIP)
        acc_v[strip, :] = gelu_slope(hid_v[tp // 2, strip, :].astype(F32))

    for copy in n_copies:
        copy.wait_recv()

    @pl.loop(0, spread)
    def _(p):
        slot = maps[at_place + p]
        flag = jnp.full((TILE, cols), slot, jnp.int32)
        normed_v[p] = jnp.where(
            flag >= 0, recv_n[jnp.maximum(slot, 0)].astype(F32), normed_v[p].astype(F32)
        ).astype(BF16)

    if stages:
        collect(stages - 1, True)

    for side in range(2):
        tails = [numbers[1 << bit] for bit, numbers in plan[side]]

        @pl.loop(0, half // STRIP)
        def _(j):
            here = pl.multiple_of(j * STRIP, STRIP)
            there = pl.ds(side * half + here, STRIP)
            total = part[0, there, :].astype(F32)
            for number in tails:
                total = total + later[side, number, pl.ds(here, STRIP), :].astype(F32)
            d_hid_v[there, :] = (total * acc_v[there, :]).astype(BF16)

    for copy in act_copies + dn_copies + x_copies + i_copies + n_copies:
        copy.wait_send()
    for copy in list(first_copies.values()) + list(later_copies.values()):
        copy.wait_send()


def hand_out(*refs):
    count = len(refs) // 2
    sem = refs[-1]
    copies = []
    for number in range(count):
        source, target = refs[number], refs[count + number]
        cut = source.shape[0] // 2
        for side in range(2):
            span = pl.ds(side * cut, cut)
            copies.append(
                pltpu.make_async_copy(
                    source.at[span], target.at[span], sem.at[2 * number + side]
                )
            )
    for copy in copies:
        copy.start()
    for copy in copies:
        copy.wait()


def on_device(hidden, proj_weight, proj_bias, tile_pos, text_embed, norm_gain, d_normed):
    rows, width = hidden.shape
    cols = proj_weight.shape[1]
    tokens = text_embed.shape[0]
    groups = lax.axis_size("grp")
    lanes = lax.axis_size("tp")
    assert lanes >= 2 and lanes & (lanes - 1) == 0, lanes
    tiles_dev = rows // TILE
    spread = tokens // TILE
    capacity = max(2, (tiles_dev + groups - 1) // groups)
    slots = groups * capacity
    maps = tile_maps(tile_pos, groups, tiles_dev, spread, capacity)
    any_spec = pl.BlockSpec(memory_space=pl.ANY)
    vmem_spec = pl.BlockSpec(memory_space=pltpu.VMEM)
    half = rows // 2
    kept = max(1, lanes // 2 - 1)

    def vmem(*shape, dtype=BF16):
        return pltpu.VMEM(shape, dtype)

    def sems(*shape):
        return pltpu.SemaphoreType.DMA(shape)

    tiled = (spread, TILE, cols)
    normed, d_text, d_hidden = pl.pallas_call(
        functools.partial(kernel, groups, lanes, capacity),
        out_shape=(
            vmem(*tiled),
            vmem(*tiled),
            vmem(rows, cols),
        ),
        in_specs=[
            pl.BlockSpec(memory_space=pltpu.SMEM),
            any_spec, any_spec, vmem_spec, vmem_spec, any_spec, any_spec,
        ],
        out_specs=(vmem_spec, vmem_spec, vmem_spec),
        scratch_shapes=[
            vmem(lanes // 2, rows, cols),
            vmem(lanes, cols, cols),
            vmem(lanes // 2, rows, cols),
            vmem(lanes // 2, rows, cols),
            vmem(rows, cols, dtype=F32),
            vmem(rows, cols),
            vmem(rows, cols),
            vmem(*tiled),
            vmem(*tiled),
            vmem(slots, TILE, cols),
            vmem(slots, TILE, cols),
            vmem(tiles_dev, TILE, cols),
            vmem(slots, TILE, cols),
            vmem(slots, TILE, cols),
            vmem(rows, LANES, dtype=F32),
            vmem(tokens, LANES, dtype=F32),
            vmem(TILE, rows, dtype=F32),
            vmem(TILE, tokens, dtype=F32),
            vmem(lanes - 1, TILE, rows, dtype=F32),
            vmem(lanes - 1, TILE, tokens, dtype=F32),
            vmem(rows, LANES, dtype=F32),
            vmem(tokens, LANES, dtype=F32),
            vmem(lanes, rows, cols),
            vmem(lanes // 2, rows, cols),
            vmem(2, kept, half, cols),
            sems(2), sems(lanes // 2), sems(lanes), sems(lanes // 2), sems(lanes // 2),
            sems(groups - 1), sems(groups - 1), sems(groups - 1), sems(groups - 1),
            sems(lanes - 1), sems(lanes - 1), sems(lanes - 1), sems(lanes - 1),
            sems(lanes // 2), sems(lanes // 2), sems(2, kept), sems(2, kept),
        ],
        compiler_params=pltpu.CompilerParams(
            collective_id=0, has_side_effects=True, vmem_limit_bytes=58 * 1024 * 1024
        ),
        cost_estimate=pl.CostEstimate(
            flops=4 * rows * width * cols,
            bytes_accessed=2 * (width * cols + rows * width + 5 * tokens * cols),
            transcendentals=rows * width // 2,
        ),
        name="projector_norm",
    )(
        maps, hidden, proj_weight, proj_bias.reshape(1, cols), norm_gain.reshape(1, cols),
        text_embed.reshape(tiled), d_normed.reshape(tiled),
    )
    normed, d_text, d_hidden = pl.pallas_call(
        hand_out,
        out_shape=(
            jax.ShapeDtypeStruct(tiled, BF16),
            jax.ShapeDtypeStruct(tiled, BF16),
            jax.ShapeDtypeStruct((rows, cols), BF16),
        ),
        in_specs=[any_spec] * 3,
        out_specs=(any_spec,) * 3,
        scratch_shapes=[sems(6)],
        compiler_params=pltpu.CompilerParams(vmem_limit_bytes=1024 * 1024),
        name="hand_out",
    )(normed, d_text, d_hidden)
    return (normed.reshape(tokens, cols), d_text.reshape(tokens, cols), d_hidden)


def solution(mesh):
    in_specs = (
        P("grp", None),
        P(None, "tp"),
        P("tp"),
        P(),
        P("grp", "tp"),
        P("tp"),
        P("grp", "tp"),
    )
    out_specs = (P("grp", "tp"), P("grp", "tp"), P("grp", "tp"))
    return jax.shard_map(
        on_device, mesh=mesh, in_specs=in_specs, out_specs=out_specs, check_vma=False
    )
```
